512 devices in a mesh: fsdp: 64 (over y, z), layer: 8 (over x, core).
Axes of the slice: x: 4, y: 4, z: 16, core: 2. Of those that a mesh axis runs over, the one named last changes fastest.
Arguments:
- pseudo_gradient: bfloat16 [1024, 16, 4096], P('fsdp', 'layer'), parts along dimension 1, may hold values from -6 to 6
- left_root: bfloat16 [64, 8192, 1024], P('fsdp', 'layer'), parts along dimension 1, may hold values from -1 to 4
- right_root: bfloat16 [64, 1024, 128], P('fsdp', 'layer'), parts along dimension 1, may hold values from -1 to 4
Outputs:
- update: bfloat16 [1024, 16, 4096], P('fsdp', 'layer'), parts along dimension 1
The draws below stay inside these ranges and needn't reach their ends.
There are 8 independent parts, one for each index of `layer`. The reference program is written for one: setup_inputs(seed, part) draws one part's arguments, and reference() takes and returns one part's arrays. A program takes and returns all parts, laid end to end along the dimension named above; each array names one. Nothing has to cross between parts.
All inputs are finite; a program needn't handle non-finite values.
Results may differ from the reference program's by a relative error of at most 0.0049.
Values may be sent and summed in bfloat16 or wider, within the bound.
A program may use at most 64 MiB of HBM per device.

```python
import math
import jax
import jax.numpy as jnp
from jax import lax

BLK = 1024
BLOCKS = 2
HD = 128
HEADS = 32
UNITS = 64
COLS = 4096


def draw_left_root(key, part):
    key = jax.random.fold_in(key, 11)
    key_entries, key_diagonal = jax.random.split(key)
    entries = jax.random.truncated_normal(key_entries, -6.0, 6.0, (UNITS, BLK, BLK), jnp.float32)
    diagonal = jnp.exp(jax.random.uniform(key_diagonal, (UNITS, BLK), jnp.float32, math.log(1.5), math.log(3.0)))
    off_diag = (entries + jnp.swapaxes(entries, 1, 2)) * (0.5 / math.sqrt(2.0 * BLK))
    identity = jnp.eye(BLK, dtype=bool)
    return jnp.where(identity[None, :, :], diagonal[:, :, None], off_diag).astype(jnp.bfloat16)


def draw_right_root(key, part):
    key = jax.random.fold_in(key, 23)
    key_entries, key_diagonal = jax.random.split(key)
    entries = jax.random.truncated_normal(key_entries, -6.0, 6.0, (UNITS, HD, HD), jnp.float32)
    diagonal = jnp.exp(jax.random.uniform(key_diagonal, (UNITS, HD), jnp.float32, math.log(1.5), math.log(3.0)))
    off_diag = (entries + jnp.swapaxes(entries, 1, 2)) * (0.5 / math.sqrt(2.0 * HD))
    identity = jnp.eye(HD, dtype=bool)
    return jnp.where(identity[None, :, :], diagonal[:, :, None], off_diag).astype(jnp.bfloat16)


def block_levels(rng, shape, cuts, smallest, top_value):
    def one(position, parts):
        heights = jax.random.uniform(jax.random.fold_in(jax.random.fold_in(rng, 6), position), (parts,), jnp.float32, smallest / len(cuts), top_value / len(cuts))
        return jnp.repeat(jnp.exp(heights), shape[position] // parts).reshape((-1,) + (1,) * (len(shape) - position - 1))

    factor_of = one(*cuts[0])
    for cut in cuts[1:]:
        factor_of = factor_of * one(*cut)
    return factor_of


def centred(stream_key, dims, scale, limit, cuts=(), held_as=jnp.bfloat16):
    factor_of = block_levels(stream_key, dims, cuts, -0.22, 0.18) if cuts else 1.0
    values = jax.random.normal(stream_key, dims, jnp.float32) * scale * factor_of
    return jnp.minimum(jnp.maximum(values, -limit), limit).astype(held_as)


def setup_inputs(seed: int = 0, part: int = 0) -> dict:
    splits = jax.random.split(jax.random.key(seed), 4)
    part_keys = jax.random.split(jax.random.fold_in(splits[3], part), 4)
    pseudo_gradient = centred(part_keys[0], (BLK, BLOCKS, COLS), 1.0, 6.0, ((0, 64),))
    left_root = draw_left_root(jax.random.fold_in(jax.random.fold_in(splits[3], part), 71), part)
    right_root = draw_right_root(jax.random.fold_in(jax.random.fold_in(splits[3], part), 71), part)
    return dict(pseudo_gradient=pseudo_gradient, left_root=left_root, right_root=right_root)


def apply_left(operands):
    root_block, column_block = operands
    return jnp.dot(root_block, column_block, preferred_element_type=jnp.float32).astype(jnp.bfloat16)


def reference(pseudo_gradient, left_root, right_root):
    grad_units = pseudo_gradient.reshape(BLK, UNITS, HD).astype(jnp.float32)
    right_part = jnp.einsum("rud,ude->rue", grad_units, right_root.astype(jnp.float32)).astype(jnp.bfloat16)
    updated = lax.map(apply_left, (left_root, jnp.swapaxes(right_part, 0, 1)))
    return jnp.swapaxes(updated, 0, 1).reshape(BLK, BLOCKS, HEADS * HD)
```

```python
import jax
import jax.numpy as jnp
from jax import lax
from jax.sharding import PartitionSpec as P

HD = 128


def shards(pseudo_gradient, left_root, right_root):
    local_rows = pseudo_gradient.shape[0]
    pieces = pseudo_gradient.reshape(local_rows, -1, HD)
    block = lax.all_to_all(pieces, "fsdp", split_axis=1, concat_axis=0, tiled=True)[:, 0, :]
    right = jnp.dot(block, right_root[0], preferred_element_type=jnp.float32).astype(jnp.bfloat16)
    update = jnp.dot(left_root[0], right, preferred_element_type=jnp.float32).astype(jnp.bfloat16)
    returned = lax.all_to_all(update[:, None, :], "fsdp", split_axis=0, concat_axis=1, tiled=True)
    return returned.reshape(pseudo_gradient.shape)


def solution(mesh):
    in_specs = (P("fsdp", "layer", None), P("fsdp", "layer", None), P("fsdp", "layer", None))
    out_specs = P("fsdp", "layer", None)
    return jax.shard_map(shards, mesh=mesh, in_specs=in_specs, out_specs=out_specs, check_vma=False)
```

```python
import jax
import jax.numpy as jnp
from jax import lax
from jax.experimental import pallas as pl
from jax.experimental.pallas import tpu as pltpu
from jax.sharding import PartitionSpec as P

HD = 128
RING = 16
MESH = pl.DeviceIdType.MESH


def partner(me, n, i):
    turn, dy = i // (n // RING), (i + 1) % (n // RING)
    half = (turn + 1) // 2
    dz = RING // 2 + half * (2 * (turn % 2) - 1)
    row, col = me // RING, me % RING
    return (row + dy) % (n // RING) * RING + (col + dz + RING) % RING


def kernel(n, pg_ref, left_ref, right_ref, out_ref, sent, block, left, update, local_sem, send_sem, recv_sem):
    me = lax.axis_index("fsdp")
    rows = pg_ref.shape[0]
    heads = n // pg_ref.shape[1]

    barrier = pltpu.get_barrier_semaphore()

    def greet(i, carry):
        pl.semaphore_signal(barrier, inc=1, device_id={"fsdp": partner(me, n, i)}, device_id_type=MESH)
        return carry

    lax.fori_loop(0, n - 1, greet, 0)
    load = pltpu.make_async_copy(left_ref.at[0], left, local_sem.at[0])
    load.start()
    for b in range(2):
        for h in range(heads):
            sent[b * heads + h] = pg_ref[:, b, h * HD:(h + 1) * HD]
    pl.semaphore_wait(barrier, n - 1)

    def exchange(phase, source, target):
        own = pltpu.make_async_copy(source.at[me], target.at[me], recv_sem.at[phase])
        own.start()

        def send(i, carry):
            to = partner(me, n, i)
            pltpu.make_async_remote_copy(
                src_ref=source.at[to],
                dst_ref=target.at[me],
                send_sem=send_sem.at[phase],
                recv_sem=recv_sem.at[phase],
                device_id={"fsdp": to},
                device_id_type=MESH,
            ).start()
            return carry

        lax.fori_loop(0, n - 1, send, 0)
        pltpu.make_async_copy(source, target, recv_sem.at[phase]).wait()

    exchange(0, sent, block)
    scaled = jnp.dot(block[...].reshape(n * rows, HD), right_ref[0], preferred_element_type=jnp.float32)
    scaled = scaled.astype(jnp.bfloat16)
    load.wait()
    product = jnp.dot(left[...], scaled, preferred_element_type=jnp.float32)
    update[...] = product.astype(jnp.bfloat16).reshape(n, rows, HD)
    exchange(1, update, out_ref)
    for phase in range(2):
        part = sent.at[pl.ds(0, n - 1)]
        pltpu.make_async_copy(part, part, send_sem.at[phase]).wait()


def solution(mesh):
    n = mesh.shape["fsdp"]

    def shards(pseudo_gradient, left_root, right_root):
        rows, blocks, cols = pseudo_gradient.shape
        units = jax.ShapeDtypeStruct((n, rows, HD), jnp.bfloat16)
        vmem = pl.BlockSpec(memory_space=pltpu.VMEM)
        returned = pl.pallas_call(
            lambda *refs: kernel(n, *refs),
            out_shape=units,
            in_specs=[vmem, pl.BlockSpec(memory_space=pl.ANY), vmem],
            out_specs=vmem,
            scratch_shapes=[
                pltpu.VMEM(units.shape, units.dtype),
                pltpu.VMEM(units.shape, units.dtype),
                pltpu.VMEM(left_root.shape[1:], units.dtype),
                pltpu.VMEM(units.shape, units.dtype),
                pltpu.SemaphoreType.DMA((1,)),
                pltpu.SemaphoreType.DMA((2,)),
                pltpu.SemaphoreType.DMA((2,)),
            ],
            compiler_params=pltpu.CompilerParams(
                collective_id=0, has_side_effects=True, vmem_limit_bytes=60 * 1024 * 1024
            ),
        )(pseudo_gradient, left_root, right_root)
        returned = returned.reshape(blocks, cols // HD, rows, HD)
        return returned.transpose(2, 0, 1, 3).reshape(pseudo_gradient.shape)

    specs = P("fsdp", "layer", None)
    return jax.shard_map(shards, mesh=mesh, in_specs=(specs,) * 3, out_specs=specs, check_vma=False)
```

```python
import jax
import jax.numpy as jnp
from jax import lax
from jax.experimental import pallas as pl
from jax.experimental.pallas import tpu as pltpu
from jax.sharding import PartitionSpec as P

HD = 128
RING = 16
MESH = pl.DeviceIdType.MESH


def ring_offset(turn):
    half = (turn + 1) // 2
    return (RING // 2 + half * (2 * (turn % 2) - 1) + RING) % RING


def kernel(n, pg_ref, left_ref, right_ref, out_ref, raw, sent, block, left, right, update, back, load_sem, send_sem,
           block_sem, back_sem):
    me = lax.axis_index("fsdp")
    layer = lax.axis_index("layer")
    rows, blocks, _ = pg_ref.shape
    heads = n // blocks
    tall = n // RING
    my_row, my_col = me // RING, me % RING
    mine = (my_row + my_col + layer) % 2

    def device(dy, dz):
        return (my_row + dy) % tall * RING + (my_col + dz) % RING

    def first_partner(i):
        place = i + (1 - mine) * ((i + 1) // (n // 2))
        odd = (mine + place // (n // 2)) % 2
        place = place % (n // 2)
        dz = ring_offset(place // 2)
        return device((odd + dz) % 2 + 2 * (1 - place % 2), dz)

    barrier = pltpu.get_barrier_semaphore()

    def greet(i, carry):
        to = device((i + 1) % tall, ring_offset(i // tall))
        pl.semaphore_signal(barrier, inc=1, device_id={"fsdp": to}, device_id_type=MESH)
        return carry

    lax.fori_loop(0, n - 1, greet, 0)
    loads = [
        pltpu.make_async_copy(pg_ref, raw, load_sem.at[0]),
        pltpu.make_async_copy(right_ref.at[0], right, load_sem.at[1]),
        pltpu.make_async_copy(left_ref.at[0], left, load_sem.at[2]),
    ]
    for load in loads:
        load.start()
    loads[0].wait()
    for h in range(heads):
        pair = raw[:, :, h * HD:(h + 1) * HD].astype(jnp.float32)
        for b in range(blocks):
            sent[b * heads + h] = pair[:, b, :].astype(jnp.bfloat16)
    pl.semaphore_wait(barrier, n - 1)

    def push(source, target, to, phase, sem):
        pltpu.make_async_remote_copy(
            src_ref=source.at[to],
            dst_ref=target.at[me],
            send_sem=send_sem.at[phase],
            recv_sem=sem,
            device_id={"fsdp": to},
            device_id_type=MESH,
        ).start()

    def send_rows(i, carry):
        push(sent, block, first_partner(i), 0, block_sem.at[0])
        return carry

    lax.fori_loop(0, n - 1, send_rows, 0)
    pltpu.make_async_copy(sent.at[me], block.at[me], block_sem.at[0]).start()
    loads[1].wait()
    loads[2].wait()
    pltpu.make_async_copy(sent, block, block_sem.at[0]).wait()
    scaled = jnp.dot(block[...].reshape(n * rows, HD), right[...], preferred_element_type=jnp.float32)
    scaled = scaled.astype(jnp.bfloat16)
    group = RING * rows
    for turn in range(tall):
        dy = (turn + 1) % tall
        row = (my_row + dy) % tall
        part = left[pl.ds(pl.multiple_of(row * group, group), group), :]
        product = jnp.dot(part, scaled, preferred_element_type=jnp.float32)
        update[pl.ds(row * RING, RING)] = product.astype(jnp.bfloat16).reshape(RING, rows, HD)

        def send_back(i, carry):
            push(update, back, device(dy, ring_offset(i)), 1, back_sem.at[mine])
            return carry

        lax.fori_loop(0, RING - (dy == 0), send_back, 0)
    pltpu.make_async_copy(update.at[me], back.at[me], back_sem.at[mine]).start()
    for c in range(2):
        half = back.at[pl.ds(0, n // 2)]
        pltpu.make_async_copy(half, half, back_sem.at[c]).wait()
        for i in range(heads // 2):
            h = 2 * i + (c + layer + i * 2 // RING) % 2
            pair = jnp.stack([back[b * heads + h] for b in range(blocks)], axis=1)
            out_ref[:, :, pl.ds(pl.multiple_of(h * HD, HD), HD)] = pair
    for phase in range(2):
        part = sent.at[pl.ds(0, n - 1)]
        pltpu.make_async_copy(part, part, send_sem.at[phase]).wait()


def solution(mesh):
    n = mesh.shape["fsdp"]

    def shards(pseudo_gradient, left_root, right_root):
        rows = pseudo_gradient.shape[0]
        units = pltpu.VMEM((n, rows, HD), jnp.bfloat16)
        args = [pltpu.with_memory_space_constraint(a, pltpu.HBM) for a in (pseudo_gradient, left_root, right_root)]
        return pl.pallas_call(
            lambda *refs: kernel(n, *refs),
            out_shape=pltpu.VMEM(pseudo_gradient.shape, pseudo_gradient.dtype),
            in_specs=[pl.BlockSpec(memory_space=pltpu.HBM)] * 3,
            out_specs=pl.BlockSpec(memory_space=pltpu.VMEM),
            scratch_shapes=[
                pltpu.VMEM(pseudo_gradient.shape, jnp.bfloat16),
                units,
                units,
                pltpu.VMEM(left_root.shape[1:], jnp.bfloat16),
                pltpu.VMEM(right_root.shape[1:], jnp.bfloat16),
                units,
                units,
                pltpu.SemaphoreType.DMA((3,)),
                pltpu.SemaphoreType.DMA((2,)),
                pltpu.SemaphoreType.DMA((1,)),
                pltpu.SemaphoreType.DMA((2,)),
            ],
            compiler_params=pltpu.CompilerParams(
                collective_id=0, has_side_effects=True, vmem_limit_bytes=32 * 1024 * 1024
            ),
        )(*args)

    specs = P("fsdp", "layer", None)
    return jax.shard_map(shards, mesh=mesh, in_specs=(specs,) * 3, out_specs=specs, check_vma=False)
```

```python
import jax
import jax.numpy as jnp
from jax import lax
from jax.experimental import pallas as pl
from jax.experimental.pallas import tpu as pltpu
from jax.sharding import PartitionSpec as P

HD = 128
RING = 16
MESH = pl.DeviceIdType.MESH


def ring_offset(turn):
    half = (turn + 1) // 2
    return (RING // 2 + half * (2 * (turn % 2) - 1) + RING) % RING


def kernel(n, pg_ref, left_ref, right_ref, out_ref, raw, sent, block, left, right, update, back, load_sem, send_sem,
           block_sem, back_sem):
    me = lax.axis_index("fsdp")
    layer = lax.axis_index("layer")
    rows, blocks, _ = pg_ref.shape
    heads = n // blocks
    tall = n // RING
    my_row, my_col = me // RING, me % RING
    mine = (my_row + my_col + layer) % 2

    def device(dy, dz):
        return (my_row + dy) % tall * RING + (my_col + dz) % RING

    def first_partner(i):
        place = i + (1 - mine) * ((i + 1) // (n // 2))
        odd = (mine + place // (n // 2)) % 2
        place = place % (n // 2)
        dz = ring_offset(place // 2)
        return device((odd + dz) % 2 + 2 * (1 - place % 2), dz)

    barrier = pltpu.get_barrier_semaphore()

    def greet(i, carry):
        to = device((i + 1) % tall, ring_offset(i // tall))
        pl.semaphore_signal(barrier, inc=1, device_id={"fsdp": to}, device_id_type=MESH)
        return carry

    lax.fori_loop(0, n - 1, greet, 0)
    loads = [
        pltpu.make_async_copy(pg_ref, raw, load_sem.at[0]),
        pltpu.make_async_copy(right_ref.at[0], right, load_sem.at[1]),
        pltpu.make_async_copy(left_ref.at[0], left, load_sem.at[2]),
    ]
    for load in loads:
        load.start()
    loads[0].wait()
    for h in range(heads):
        pair = raw[:, :, h * HD:(h + 1) * HD].astype(jnp.float32)
        for b in range(blocks):
            sent[b * heads + h] = pair[:, b, :].astype(jnp.bfloat16)
    pl.semaphore_wait(barrier, n - 1)

    def push(source, target, to, phase, sem):
        pltpu.make_async_remote_copy(
            src_ref=source.at[to],
            dst_ref=target.at[me],
            send_sem=send_sem.at[phase],
            recv_sem=sem,
            device_id={"fsdp": to},
            device_id_type=MESH,
        ).start()

    def send_rows(i, carry):
        push(sent, block, first_partner(i), 0, block_sem.at[0])
        return carry

    lax.fori_loop(0, n - 1, send_rows, 0)
    pltpu.make_async_copy(sent.at[me], block.at[me], block_sem.at[0]).start()
    loads[1].wait()
    loads[2].wait()
    pltpu.make_async_copy(sent, block, block_sem.at[0]).wait()
    scaled = jnp.dot(block[...].reshape(n * rows, HD), right[...], preferred_element_type=jnp.float32)
    scaled = scaled.astype(jnp.bfloat16)
    quarter = RING // 4
    for q in range(4):
        part = left[...].reshape(tall, 4, quarter * rows, n * rows)[:, q].reshape(-1, n * rows)
        product = jnp.dot(part, scaled, preferred_element_type=jnp.float32).astype(jnp.bfloat16)
        for y in range(tall):
            first = y * RING + q * quarter
            update[first:first + quarter] = product.reshape(tall, quarter, rows, HD)[y]

        def send_back(i, carry):
            to = (my_row + i + 1) % tall * RING + q * quarter + (i // tall + my_col) % quarter

            @pl.when(to != me)
            def _():
                push(update, back, to, 1, back_sem.at[mine])

            return carry

        lax.fori_loop(0, quarter * tall, send_back, 0)
    pltpu.make_async_copy(update.at[me], back.at[me], back_sem.at[mine]).start()
    for c in range(2):
        half = back.at[pl.ds(0, n // 2)]
        pltpu.make_async_copy(half, half, back_sem.at[c]).wait()
        for i in range(heads // 2):
            h = 2 * i + (c + layer + i * 2 // RING) % 2
            pair = jnp.stack([back[b * heads + h] for b in range(blocks)], axis=1)
            out_ref[:, :, pl.ds(pl.multiple_of(h * HD, HD), HD)] = pair
    for phase in range(2):
        part = sent.at[pl.ds(0, n - 1)]
        pltpu.make_async_copy(part, part, send_sem.at[phase]).wait()


def solution(mesh):
    n = mesh.shape["fsdp"]

    def shards(pseudo_gradient, left_root, right_root):
        rows = pseudo_gradient.shape[0]
        units = pltpu.VMEM((n, rows, HD), jnp.bfloat16)
        args = [pltpu.with_memory_space_constraint(a, pltpu.HBM) for a in (pseudo_gradient, left_root, right_root)]
        return pl.pallas_call(
            lambda *refs: kernel(n, *refs),
            out_shape=pltpu.VMEM(pseudo_gradient.shape, pseudo_gradient.dtype),
            in_specs=[pl.BlockSpec(memory_space=pltpu.HBM)] * 3,
            out_specs=pl.BlockSpec(memory_space=pltpu.VMEM),
            scratch_shapes=[
                pltpu.VMEM(pseudo_gradient.shape, jnp.bfloat16),
                units,
                units,
                pltpu.VMEM(left_root.shape[1:], jnp.bfloat16),
                pltpu.VMEM(right_root.shape[1:], jnp.bfloat16),
                units,
                units,
                pltpu.SemaphoreType.DMA((3,)),
                pltpu.SemaphoreType.DMA((2,)),
                pltpu.SemaphoreType.DMA((1,)),
                pltpu.SemaphoreType.DMA((2,)),
            ],
            compiler_params=pltpu.CompilerParams(
                collective_id=0, has_side_effects=True, vmem_limit_bytes=32 * 1024 * 1024
            ),
        )(*args)

    specs = P("fsdp", "layer", None)
    return jax.shard_map(shards, mesh=mesh, in_specs=(specs,) * 3, out_specs=specs, check_vma=False)
```

```python
import jax
import jax.numpy as jnp
from jax import lax
from jax.experimental import pallas as pl
from jax.experimental.pallas import tpu as pltpu
from jax.sharding import PartitionSpec as P

HD = 128
RING = 16
MESH = pl.DeviceIdType.MESH


def ring_offset(turn):
    half = (turn + 1) // 2
    return (RING // 2 + half * (2 * (turn % 2) - 1) + RING) % RING


def kernel(n, pg_ref, left_ref, right_ref, out_ref, raw, sent, block, left, right, update, back, load_sem, send_sem,
           block_sem, back_sem):
    me = lax.axis_index("fsdp")
    layer = lax.axis_index("layer")
    rows, blocks, _ = pg_ref.shape
    heads = n // blocks
    tall = n // RING
    my_row, my_col = me // RING, me % RING
    mine = (my_row + my_col + layer) % 2

    def device(dy, dz):
        return (my_row + dy) % tall * RING + (my_col + dz) % RING

    def first_partner(i):
        place = i + (1 - mine) * ((i + 1) // (n // 2))
        odd = (mine + place // (n // 2)) % 2
        place = place % (n // 2)
        dz = ring_offset(place // 2)
        return device((odd + dz) % 2 + 2 * (1 - place % 2), dz)

    barrier = pltpu.get_barrier_semaphore()

    def greet(i, carry):
        to = device((i + 1) % tall, ring_offset(i // tall))
        pl.semaphore_signal(barrier, inc=1, device_id={"fsdp": to}, device_id_type=MESH)
        return carry

    lax.fori_loop(0, n - 1, greet, 0)
    loads = [
        pltpu.make_async_copy(pg_ref, raw, load_sem.at[0]),
        pltpu.make_async_copy(right_ref.at[0], right, load_sem.at[1]),
        pltpu.make_async_copy(left_ref.at[0], left, load_sem.at[2]),
    ]
    for load in loads:
        load.start()
    loads[0].wait()
    for h in range(heads):
        pair = raw[:, :, h * HD:(h + 1) * HD].astype(jnp.float32)
        for b in range(blocks):
            sent[b * heads + h] = pair[:, b, :].astype(jnp.bfloat16)
    pl.semaphore_wait(barrier, n - 1)

    def push(source, target, to, sent_sem, sem):
        pltpu.make_async_remote_copy(
            src_ref=source.at[to],
            dst_ref=target.at[me],
            send_sem=sent_sem,
            recv_sem=sem,
            device_id={"fsdp": to},
            device_id_type=MESH,
        ).start()

    def send_rows(i, carry):
        push(sent, block, first_partner(i), send_sem.at[0], block_sem.at[0])
        return carry

    lax.fori_loop(0, n - 1, send_rows, 0)
    pltpu.make_async_copy(sent.at[me], block.at[me], block_sem.at[0]).start()
    loads[1].wait()
    loads[2].wait()
    pltpu.make_async_copy(sent, block, block_sem.at[0]).wait()
    scaled = jnp.dot(block[...].reshape(n * rows, HD), right[...], preferred_element_type=jnp.float32)
    scaled = scaled.astype(jnp.bfloat16)
    quarter = RING // 4
    group = quarter * tall
    core = layer % 2

    def settle(q):
        here = jnp.where(my_col // quarter == q, 1, 0)
        for less in range(2):
            part = sent.at[pl.ds(0, group - less)]

            @pl.when(here == less)
            def _():
                pltpu.make_async_copy(part, part, send_sem.at[1 + q]).wait()

    for q in range(4):
        part = [left[pl.ds((y * RING + q * quarter) * rows, quarter * rows), :] for y in range(tall)]
        product = jnp.dot(jnp.concatenate(part), scaled, preferred_element_type=jnp.float32).astype(jnp.bfloat16)
        for y in range(tall):
            update[pl.ds(y * RING + q * quarter, quarter)] = product.reshape(tall, quarter, rows, HD)[y]
        if q >= 2:
            pl.when(core == 1)(lambda q=q: settle(q - 2))

        def send_back(i, carry):
            to = i // quarter * RING + q * quarter + (i + my_col) % quarter

            @pl.when(to != me)
            def _():
                push(update, back, to, send_sem.at[1 + q], back_sem.at[mine])

            return carry

        lax.fori_loop(0, group, send_back, 0)
    pltpu.make_async_copy(update.at[me], back.at[me], back_sem.at[mine]).start()
    for c in range(2):
        half = back.at[pl.ds(0, n // 2)]
        pltpu.make_async_copy(half, half, back_sem.at[c]).wait()
        for i in range(heads // 2):
            h = 2 * i + (c + layer + i * 2 // RING) % 2
            pair = jnp.stack([back[b * heads + h] for b in range(blocks)], axis=1)
            out_ref[:, :, pl.ds(pl.multiple_of(h * HD, HD), HD)] = pair
    part = sent.at[pl.ds(0, n - 1)]
    pltpu.make_async_copy(part, part, send_sem.at[0]).wait()
    for q in range(2):
        pl.when(core == 0)(lambda q=q: settle(q))
    for q in range(2, 4):
        settle(q)


def solution(mesh):
    n = mesh.shape["fsdp"]

    def shards(pseudo_gradient, left_root, right_root):
        rows = pseudo_gradient.shape[0]
        units = pltpu.VMEM((n, rows, HD), jnp.bfloat16)
        args = [pltpu.with_memory_space_constraint(a, pltpu.HBM) for a in (pseudo_gradient, left_root, right_root)]
        return pl.pallas_call(
            lambda *refs: kernel(n, *refs),
            out_shape=pltpu.VMEM(pseudo_gradient.shape, pseudo_gradient.dtype),
            in_specs=[pl.BlockSpec(memory_space=pltpu.HBM)] * 3,
            out_specs=pl.BlockSpec(memory_space=pltpu.VMEM),
            scratch_shapes=[
                pltpu.VMEM(pseudo_gradient.shape, jnp.bfloat16),
                units,
                units,
                pltpu.VMEM(left_root.shape[1:], jnp.bfloat16),
                pltpu.VMEM(right_root.shape[1:], jnp.bfloat16),
                units,
                units,
                pltpu.SemaphoreType.DMA((3,)),
                pltpu.SemaphoreType.DMA((5,)),
                pltpu.SemaphoreType.DMA((1,)),
                pltpu.SemaphoreType.DMA((2,)),
            ],
            compiler_params=pltpu.CompilerParams(
                collective_id=0, has_side_effects=True, vmem_limit_bytes=32 * 1024 * 1024
            ),
        )(*args)

    specs = P("fsdp", "layer", None)
    return jax.shard_map(shards, mesh=mesh, in_specs=(specs,) * 3, out_specs=specs, check_vma=False)
```

```python
import jax
import jax.numpy as jnp
from jax import lax
from jax.experimental import pallas as pl
from jax.experimental.pallas import tpu as pltpu
from jax.sharding import PartitionSpec as P

HD = 128
RING = 16
MESH = pl.DeviceIdType.MESH


def ring_offset(turn):
    half = (turn + 1) // 2
    return (RING // 2 + half * (2 * (turn % 2) - 1) + RING) % RING


def kernel(n, pg_ref, left_ref, right_ref, out_ref, raw, sent, block, left, right, update, back, load_sem, send_sem,
           block_sem, back_sem):
    me = lax.axis_index("fsdp")
    layer = lax.axis_index("layer")
    rows, blocks, _ = pg_ref.shape
    heads = n // blocks
    tall = n // RING
    my_row, my_col = me // RING, me % RING
    mine = (my_row + my_col + layer) % 2

    def device(dy, dz):
        return (my_row + dy) % tall * RING + (my_col + dz) % RING

    def first_partner(i):
        place = i + (1 - mine) * ((i + 1) // (n // 2))
        odd = (mine + place // (n // 2)) % 2
        place = place % (n // 2)
        dz = ring_offset(place // 2)
        return device((odd + dz) % 2 + 2 * (1 - place % 2), dz)

    barrier = pltpu.get_barrier_semaphore()

    def greet(i, carry):
        to = device((i + 1) % tall, ring_offset(i // tall))
        pl.semaphore_signal(barrier, inc=1, device_id={"fsdp": to}, device_id_type=MESH)
        return carry

    lax.fori_loop(0, n - 1, greet, 0)
    loads = [
        pltpu.make_async_copy(pg_ref, raw, load_sem.at[0]),
        pltpu.make_async_copy(right_ref.at[0], right, load_sem.at[1]),
        pltpu.make_async_copy(left_ref.at[0], left, load_sem.at[2]),
    ]
    for load in loads:
        load.start()
    loads[0].wait()
    for h in range(heads):
        pair = raw[:, :, h * HD:(h + 1) * HD].astype(jnp.float32)
        for b in range(blocks):
            sent[b * heads + h] = pair[:, b, :].astype(jnp.bfloat16)
    pl.semaphore_wait(barrier, n - 1)

    def push(source, target, to, sent_sem, sem):
        pltpu.make_async_remote_copy(
            src_ref=source.at[to],
            dst_ref=target.at[me],
            send_sem=sent_sem,
            recv_sem=sem,
            device_id={"fsdp": to},
            device_id_type=MESH,
        ).start()

    def send_rows(i, carry):
        push(sent, block, first_partner(i), send_sem.at[0], block_sem.at[0])
        return carry

    lax.fori_loop(0, n - 1, send_rows, 0)
    pltpu.make_async_copy(sent.at[me], block.at[me], block_sem.at[0]).start()
    loads[1].wait()
    loads[2].wait()
    pltpu.make_async_copy(sent, block, block_sem.at[0]).wait()
    scaled = jnp.dot(block[...].reshape(n * rows, HD), right[...], preferred_element_type=jnp.float32)
    scaled = scaled.astype(jnp.bfloat16)
    quarter = RING // 4
    group = quarter * tall
    core = layer % 2

    def settle(q):
        here = jnp.where(my_col // quarter == q, 1, 0)
        for less in range(2):
            part = sent.at[pl.ds(0, group - less)]

            @pl.when(here == less)
            def _():
                pltpu.make_async_copy(part, part, send_sem.at[1 + q]).wait()

    for q in range(4):
        part = [left[pl.ds((y * RING + q * quarter) * rows, quarter * rows), :] for y in range(tall)]
        product = jnp.dot(jnp.concatenate(part), scaled, preferred_element_type=jnp.float32).astype(jnp.bfloat16)
        for y in range(tall):
            update[pl.ds(y * RING + q * quarter, quarter)] = product.reshape(tall, quarter, rows, HD)[y]
        if q >= 2:
            pl.when(core == 1)(lambda q=q: settle(q - 2))

        def send_back(i, carry):
            to = i // quarter * RING + q * quarter + (i + my_col) % quarter

            @pl.when(to != me)
            def _():
                push(update, back, to, send_sem.at[1 + q], back_sem.at[mine])

            return carry

        lax.fori_loop(0, group, send_back, 0)
    pltpu.make_async_copy(update.at[me], back.at[me], back_sem.at[mine]).start()
    for c in range(2):
        half = back.at[pl.ds(0, n // 2)]
        pltpu.make_async_copy(half, half, back_sem.at[c]).wait()
        for i in range(heads // 2):
            h = 2 * i + (c + layer + i * 2 // RING) % 2
            pair = jnp.stack([back[b * heads + h] for b in range(blocks)], axis=1)
            out_ref[:, :, pl.ds(pl.multiple_of(h * HD, HD), HD)] = pair
    part = sent.at[pl.ds(0, n - 1)]
    pltpu.make_async_copy(part, part, send_sem.at[0]).wait()
    for q in range(2):
        pl.when(core == 0)(lambda q=q: settle(q))
    for q in range(2, 4):
        settle(q)


def store(value_ref, out_ref, sem):
    rows = out_ref.shape[0] // 2
    copies = []
    for c in range(2):
        part = pl.ds(c * rows, rows)
        copies.append(pltpu.make_async_copy(value_ref.at[part], out_ref.at[part], sem.at[c]))
    for copy in copies:
        copy.start()
    for copy in copies:
        copy.wait()


def solution(mesh):
    n = mesh.shape["fsdp"]

    def shards(pseudo_gradient, left_root, right_root):
        rows = pseudo_gradient.shape[0]
        units = pltpu.VMEM((n, rows, HD), jnp.bfloat16)
        args = [pltpu.with_memory_space_constraint(a, pltpu.HBM) for a in (pseudo_gradient, left_root, right_root)]
        result = pl.pallas_call(
            lambda *refs: kernel(n, *refs),
            out_shape=pltpu.VMEM(pseudo_gradient.shape, pseudo_gradient.dtype),
            in_specs=[pl.BlockSpec(memory_space=pltpu.HBM)] * 3,
            out_specs=pl.BlockSpec(memory_space=pltpu.VMEM),
            scratch_shapes=[
                pltpu.VMEM(pseudo_gradient.shape, jnp.bfloat16),
                units,
                units,
                pltpu.VMEM(left_root.shape[1:], jnp.bfloat16),
                pltpu.VMEM(right_root.shape[1:], jnp.bfloat16),
                units,
                units,
                pltpu.SemaphoreType.DMA((3,)),
                pltpu.SemaphoreType.DMA((5,)),
                pltpu.SemaphoreType.DMA((1,)),
                pltpu.SemaphoreType.DMA((2,)),
            ],
            compiler_params=pltpu.CompilerParams(
                collective_id=0, has_side_effects=True, vmem_limit_bytes=32 * 1024 * 1024
            ),
        )(*args)
        return pl.pallas_call(
            store,
            out_shape=pltpu.HBM(result.shape, result.dtype),
            in_specs=[pl.BlockSpec(memory_space=pltpu.VMEM)],
            out_specs=pl.BlockSpec(memory_space=pltpu.HBM),
            scratch_shapes=[pltpu.SemaphoreType.DMA((2,))],
        )(pltpu.with_memory_space_constraint(result, pltpu.VMEM))

    specs = P("fsdp", "layer", None)
    return jax.shard_map(shards, mesh=mesh, in_specs=(specs,) * 3, out_specs=specs, check_vma=False)
```

```python
import jax
import jax.numpy as jnp
from jax import lax
from jax.experimental import pallas as pl
from jax.experimental.pallas import tpu as pltpu
from jax.sharding import PartitionSpec as P

HD = 128
RING = 16
MESH = pl.DeviceIdType.MESH


def ring_offset(turn):
    half = (turn + 1) // 2
    return (RING // 2 + half * (2 * (turn % 2) - 1) + RING) % RING


def kernel(n, pg_ref, left_ref, right_ref, out_ref, raw, sent, block, left, right, update, back, load_sem, send_sem,
           block_sem, back_sem):
    me = lax.axis_index("fsdp")
    layer = lax.axis_index("layer")
    rows, blocks, _ = pg_ref.shape
    heads = n // blocks
    tall = n // RING
    my_row, my_col = me // RING, me % RING
    mine = (my_row + my_col + layer) % 2

    def device(dy, dz):
        return (my_row + dy) % tall * RING + (my_col + dz) % RING

    def first_partner(i):
        place = i + (1 - mine) * ((i + 1) // (n // 2))
        odd = (mine + place // (n // 2)) % 2
        place = place % (n // 2)
        dz = ring_offset(place // 2)
        return device((odd + dz) % 2 + 2 * (1 - place % 2), dz)

    barrier = pltpu.get_barrier_semaphore()

    def greet(i, carry):
        to = device((i + 1) % tall, ring_offset(i // tall))
        pl.semaphore_signal(barrier, inc=1, device_id={"fsdp": to}, device_id_type=MESH)
        return carry

    lax.fori_loop(0, n - 1, greet, 0)
    loads = [
        pltpu.make_async_copy(pg_ref, raw, load_sem.at[0]),
        pltpu.make_async_copy(right_ref.at[0], right, load_sem.at[1]),
        pltpu.make_async_copy(left_ref.at[0], left, load_sem.at[2]),
    ]
    for load in loads:
        load.start()
    loads[0].wait()
    for h in range(heads):
        pair = raw[:, :, h * HD:(h + 1) * HD].astype(jnp.float32)
        for b in range(blocks):
            sent[b * heads + h] = pair[:, b, :].astype(jnp.bfloat16)
    pl.semaphore_wait(barrier, n - 1)

    def push(source, target, to, sent_sem, sem):
        pltpu.make_async_remote_copy(
            src_ref=source.at[to],
            dst_ref=target.at[me],
            send_sem=sent_sem,
            recv_sem=sem,
            device_id={"fsdp": to},
            device_id_type=MESH,
        ).start()

    def send_rows(i, carry):
        push(sent, block, first_partner(i), send_sem.at[0], block_sem.at[0])
        return carry

    lax.fori_loop(0, n - 1, send_rows, 0)
    pltpu.make_async_copy(sent.at[me], block.at[me], block_sem.at[0]).start()
    loads[1].wait()
    loads[2].wait()
    pltpu.make_async_copy(sent, block, block_sem.at[0]).wait()
    scaled = jnp.dot(block[...].reshape(n * rows, HD), right[...], preferred_element_type=jnp.float32)
    scaled = scaled.astype(jnp.bfloat16)
    quarter = RING // 4
    group = quarter * tall
    core = layer % 2 * jnp.where(my_col >= quarter, 1, 0)

    def settle(q):
        here = jnp.where(my_col // quarter == q, 1, 0)
        for less in range(2):
            part = sent.at[pl.ds(0, group - less)]

            @pl.when(here == less)
            def _():
                pltpu.make_async_copy(part, part, send_sem.at[1 + q]).wait()

    for q in range(4):
        part = [left[pl.ds((y * RING + q * quarter) * rows, quarter * rows), :] for y in range(tall)]
        product = jnp.dot(jnp.concatenate(part), scaled, preferred_element_type=jnp.float32).astype(jnp.bfloat16)
        for y in range(tall):
            update[pl.ds(y * RING + q * quarter, quarter)] = product.reshape(tall, quarter, rows, HD)[y]
        if q >= 2:
            pl.when(core == 1)(lambda q=q: settle(q - 2))

        def send_back(i, carry):
            to = i // quarter * RING + q * quarter + (i + my_col) % quarter

            @pl.when(to != me)
            def _():
                push(update, back, to, send_sem.at[1 + q], back_sem.at[mine])

            return carry

        lax.fori_loop(0, group, send_back, 0)
    pltpu.make_async_copy(update.at[me], back.at[me], back_sem.at[mine]).start()
    for c in range(2):
        half = back.at[pl.ds(0, n // 2)]
        pltpu.make_async_copy(half, half, back_sem.at[c]).wait()
        for i in range(heads // 2):
            h = 2 * i + (c + layer + i * 2 // RING) % 2
            pair = jnp.stack([back[b * heads + h] for b in range(blocks)], axis=1)
            out_ref[:, :, pl.ds(pl.multiple_of(h * HD, HD), HD)] = pair
    part = sent.at[pl.ds(0, n - 1)]
    pltpu.make_async_copy(part, part, send_sem.at[0]).wait()
    for q in range(2):
        pl.when(core == 0)(lambda q=q: settle(q))
    for q in range(2, 4):
        settle(q)


def store(value_ref, out_ref, sem):
    rows = out_ref.shape[0] // 2
    copies = []
    for c in range(2):
        part = pl.ds(c * rows, rows)
        copies.append(pltpu.make_async_copy(value_ref.at[part], out_ref.at[part], sem.at[c]))
    for copy in copies:
        copy.start()
    for copy in copies:
        copy.wait()


def solution(mesh):
    n = mesh.shape["fsdp"]

    def shards(pseudo_gradient, left_root, right_root):
        rows = pseudo_gradient.shape[0]
        units = pltpu.VMEM((n, rows, HD), jnp.bfloat16)
        args = [pltpu.with_memory_space_constraint(a, pltpu.HBM) for a in (pseudo_gradient, left_root, right_root)]
        result = pl.pallas_call(
            lambda *refs: kernel(n, *refs),
            out_shape=pltpu.VMEM(pseudo_gradient.shape, pseudo_gradient.dtype),
            in_specs=[pl.BlockSpec(memory_space=pltpu.HBM)] * 3,
            out_specs=pl.BlockSpec(memory_space=pltpu.VMEM),
            scratch_shapes=[
                pltpu.VMEM(pseudo_gradient.shape, jnp.bfloat16),
                units,
                units,
                pltpu.VMEM(left_root.shape[1:], jnp.bfloat16),
                pltpu.VMEM(right_root.shape[1:], jnp.bfloat16),
                units,
                units,
                pltpu.SemaphoreType.DMA((3,)),
                pltpu.SemaphoreType.DMA((5,)),
                pltpu.SemaphoreType.DMA((1,)),
                pltpu.SemaphoreType.DMA((2,)),
            ],
            compiler_params=pltpu.CompilerParams(
                collective_id=0, has_side_effects=True, vmem_limit_bytes=32 * 1024 * 1024
            ),
        )(*args)
        return pl.pallas_call(
            store,
            out_shape=pltpu.HBM(result.shape, result.dtype),
            in_specs=[pl.BlockSpec(memory_space=pltpu.VMEM)],
            out_specs=pl.BlockSpec(memory_space=pltpu.HBM),
            scratch_shapes=[pltpu.SemaphoreType.DMA((2,))],
        )(pltpu.with_memory_space_constraint(result, pltpu.VMEM))

    specs = P("fsdp", "layer", None)
    return jax.shard_map(shards, mesh=mesh, in_specs=(specs,) * 3, out_specs=specs, check_vma=False)
```
